512 devices in a mesh: tensor: 4 (over z_lo, core), context: 128 (over z_hi, x, y).
Axes of the slice: x: 4, y: 8, z: 8 (z_hi: 4, z_lo: 2; z = z_hi * 2 + z_lo), core: 2. Of those that a mesh axis runs over, the one named last changes fastest.
Arguments:
- inputs: bfloat16 [16384, 1024], P('context', 'tensor'), may hold values from -6 to 6
- gates: bfloat16 [16384, 1024], P('context', 'tensor'), may hold values from -6 to 6
- filters: float32 [16384, 256], P('context'), may hold values from -6 to 6
- skip: float32 [1024], P('tensor'), may hold values from 0.5 to 2
- out_grad: bfloat16 [16384, 1024], P('context', 'tensor'), may hold values from -6 to 6
Outputs:
- input_grad: bfloat16 [16384, 1024], P('context', 'tensor')
- gate_grad: bfloat16 [16384, 1024], P('context', 'tensor')
- filter_grad: float32 [16384, 256], P('context')
The draws below stay inside these ranges and needn't reach their ends.
All inputs are finite; a program needn't handle non-finite values.
Results may differ from the reference program's by a relative error of at most 0.0015.
Values sent between devices are 32-bit elements; how exact they have to be, the bound alone decides.
No kernel may reach another device: no remote copies, remote signals or barrier semaphores. Data moves between devices by JAX's collectives and lax.ppermute only.
A program may use at most 64 MiB of HBM per device.

```python
import math
import jax
import jax.numpy as jnp
from jax import lax

C_DEV = 256
SEQ = 16384
CHANNELS = 1024
N_TENSOR = 4


def shard_levels(own_key, shape, shards, smallest, high):
    loudness, own = 1.0, jax.random.fold_in(own_key, 6)
    for axis_at, blocks in shards:
        draws = jnp.exp(jax.random.uniform(jax.random.fold_in(own, axis_at), (blocks,), jnp.float32, smallest / len(shards), high / len(shards)))
        loudness = loudness * jnp.repeat(draws, shape[axis_at] // blocks).reshape([-1 if axis == axis_at else 1 for axis in range(len(shape))])
    return loudness


def scatter_about(key, shape, spread, limit, shards=(), held_as=jnp.bfloat16):
    entries = jax.random.normal(key, shape, jnp.float32) * spread
    if len(shards) > 0:
        entries = shard_levels(key, shape, shards, -0.22, 0.18) * entries
    return jnp.clip(entries, min=-limit, max=limit).astype(held_as)


def setup_inputs(seed: int = 0) -> dict:
    arg_keys = jax.random.split(jax.random.key(seed), 6)
    inputs = scatter_about(arg_keys[0], (SEQ, CHANNELS), 1.0, 6.0, ((0, 128), (1, 4)))
    gates = scatter_about(arg_keys[1], (SEQ, CHANNELS), 1.0, 6.0, ((0, 128), (1, 4)))
    filters = scatter_about(arg_keys[2], (SEQ, C_DEV), 1.0, 6.0, ((0, 128),), jnp.float32)
    skip = jnp.clip(jnp.exp(math.log(2.0) - 1.3862944 * jax.random.uniform(arg_keys[3], (CHANNELS,), jnp.float32) ** shard_levels(arg_keys[3], (CHANNELS,), ((0, 4),), -0.2, 0.2)), 0.5, 2.0)
    out_grad = scatter_about(arg_keys[4], (SEQ, CHANNELS), 1.0, 6.0, ((0, 128), (1, 4)))
    return dict(inputs=inputs, gates=gates, filters=filters, skip=skip, out_grad=out_grad)


def reference(inputs, gates, filters, skip, out_grad):
    length = inputs.shape[0]
    nfft = 2 * length
    factor = 1.0 / math.sqrt(length)
    filt_spec = jnp.fft.rfft(filters * factor, n=nfft, axis=0)

    def one_slab(carry, slab):
        start = (slab * C_DEV).astype(jnp.int32)
        signal = lax.dynamic_slice_in_dim(inputs, start, C_DEV, 1).astype(jnp.float32)
        gate = lax.dynamic_slice_in_dim(gates, start, C_DEV, 1).astype(jnp.float32)
        upstream = lax.dynamic_slice_in_dim(out_grad, start, C_DEV, 1).astype(jnp.float32)
        weight = lax.dynamic_slice_in_dim(skip, start, C_DEV, 0)
        mixed = upstream * gate
        sig_spec = jnp.fft.rfft(signal, n=nfft, axis=0)
        mix_spec = jnp.fft.rfft(mixed, n=nfft, axis=0)
        conv = jnp.fft.irfft(filt_spec * sig_spec, n=nfft, axis=0)[:length]
        back = jnp.fft.irfft(jnp.conj(filt_spec) * mix_spec, n=nfft, axis=0)[:length]
        shared = jnp.fft.irfft(mix_spec * jnp.conj(sig_spec), n=nfft, axis=0)[:length] * factor
        hidden = conv + weight * signal
        input_part = (back + weight * mixed).astype(jnp.bfloat16)
        gate_part = (upstream * hidden).astype(jnp.bfloat16)
        return (carry + shared, (input_part, gate_part))
    initial = jnp.zeros((length, C_DEV), jnp.float32)
    filter_grad, (input_parts, gate_parts) = lax.scan(one_slab, initial, jnp.arange(N_TENSOR, dtype=jnp.int32))
    input_grad = jnp.transpose(input_parts, (1, 0, 2)).reshape(length, N_TENSOR * C_DEV)
    gate_grad = jnp.transpose(gate_parts, (1, 0, 2)).reshape(length, N_TENSOR * C_DEV)
    return (input_grad, gate_grad, filter_grad)
```

```python
import math

import jax
import jax.numpy as jnp
import numpy as np
from jax import lax
from jax.experimental import pallas as pl
from jax.experimental.pallas import tpu as pltpu
from jax.sharding import PartitionSpec as P

N = 128
F32 = jnp.float32
BF16 = jnp.bfloat16


def tables():
    length = N * N
    index = np.arange(N)
    turn = (np.outer(4 * index + 1, index) % (4 * N)) * (2 * math.pi / (4 * N))
    first = [np.cos(turn), -np.sin(turn)]
    scale = 1.0 / (length * math.sqrt(length))
    last = [first[0].T * scale, first[1].T * scale]
    turn = np.outer(4 * index + 1, index) * (2 * math.pi / (4 * length))
    twist = [np.cos(turn), -np.sin(turn)]
    turn = (np.outer(index, index) % N) * (2 * math.pi / N)
    row = [np.cos(turn), -np.sin(turn)]
    return np.stack(first + twist + row + last).astype(np.float32)


def halves(value):
    high = value.astype(BF16)
    return high, (value - high.astype(F32)).astype(BF16)


def dot(a, b):
    return jnp.dot(a, b, preferred_element_type=F32)


def exact_dot(a, b):
    a_high, a_low = halves(a)
    b_high, b_low = halves(b)
    return dot(a_high, b_high) + (dot(a_low, b_high) + dot(a_high, b_low))


def pack_kernel(x_ref, g_ref, f_ref, o_ref, out_ref):
    x = x_ref[...].astype(F32)
    mixed = o_ref[...].astype(F32) * g_ref[...].astype(F32)
    for a, value in enumerate((x, mixed, f_ref[...])):
        for c in range(2):
            out_ref[pl.ds(2 * a + c, N, stride=6), :] = value[:, c * N : (c + 1) * N].T


def conv_kernel(in_ref, table_ref, out_ref):
    first = jnp.concatenate([table_ref[0], table_ref[1]], axis=0)
    tr, ti = table_ref[2], table_ref[3]
    rr, ri = table_ref[4], table_ref[5]
    forth = jnp.concatenate(
        [jnp.concatenate([rr, ri], axis=1), jnp.concatenate([-ri, rr], axis=1)], axis=0
    )
    back_table = jnp.concatenate(
        [jnp.concatenate([rr, -ri], axis=1), jnp.concatenate([ri, rr], axis=1)], axis=0
    )
    last = jnp.concatenate([table_ref[6], table_ref[7]], axis=1)
    field = jnp.concatenate([in_ref[pl.ds(s, N, stride=6), :] for s in range(6)], axis=1)
    spec = exact_dot(first, field)
    rows = []
    for s in range(6):
        re, im = spec[:N, s * N : (s + 1) * N], spec[N:, s * N : (s + 1) * N]
        rows.append(jnp.concatenate([re * tr - im * ti, re * ti + im * tr], axis=1))
    spec = exact_dot(jnp.concatenate(rows, axis=0), forth)

    def part(s):
        block = spec[s * N : (s + 1) * N]
        return block[:, :N], block[:, N:]

    conv, back, share = [], [], []
    for c in range(2):
        xr, xi = part(c)
        mr, mi = part(2 + c)
        fr, fi = part(4 + c)
        conv.append(jnp.concatenate([fr * xr - fi * xi, fr * xi + fi * xr], axis=1))
        back.append(jnp.concatenate([fr * mr + fi * mi, fr * mi - fi * mr], axis=1))
        share.append(jnp.concatenate([mr * xr + mi * xi, mi * xr - mr * xi], axis=1))
    spec = exact_dot(jnp.concatenate(conv + back + share, axis=0), back_table)
    columns = []
    for s in range(6):
        re, im = part(s)
        columns.append(jnp.concatenate([re * tr + im * ti, im * tr - re * ti], axis=0))
    result = exact_dot(last, jnp.concatenate(columns, axis=1))
    for s in range(6):
        out_ref[pl.ds(s, N, stride=6), :] = result[:, s * N : (s + 1) * N]


def share_kernel(in_ref, out_ref):
    for c in range(2):
        out_ref[:, c * N : (c + 1) * N] = in_ref[pl.ds(4 + c, N, stride=6), :].T


def unpack_kernel(in_ref, x_ref, g_ref, o_ref, skip_ref, input_ref, gate_ref):
    for c in range(2):
        at = slice(c * N, (c + 1) * N)
        x = x_ref[:, at].astype(F32)
        upstream = o_ref[:, at].astype(F32)
        mixed = upstream * g_ref[:, at].astype(F32)
        skip = skip_ref[:, at]
        conv = in_ref[pl.ds(c, N, stride=6), :].T
        back = in_ref[pl.ds(2 + c, N, stride=6), :].T
        input_ref[:, at] = (back + skip * mixed).astype(BF16)
        gate_ref[:, at] = (upstream * (conv + skip * x)).astype(BF16)


def call(kernel, out, *operands):
    return pl.pallas_call(
        kernel,
        out_shape=out,
        compiler_params=pltpu.CompilerParams(vmem_limit_bytes=24 << 20),
    )(*operands)


def shape(*dims, dtype=F32):
    return jax.ShapeDtypeStruct(dims, dtype)


def exchange(field):
    field = field.reshape(N, 1, 6 * N)
    field = lax.all_to_all(field, "context", split_axis=0, concat_axis=0, tiled=True)
    return field.reshape(6 * N, N)


def local(inputs, gates, filters, skip, out_grad):
    sent = call(pack_kernel, shape(6 * N, N), inputs, gates, filters, out_grad)
    taken = exchange(sent)
    sent = call(conv_kernel, shape(6 * N, N), taken, jnp.asarray(tables()))
    taken = exchange(sent)
    share = call(share_kernel, shape(N, 2 * N), taken)
    share = share + lax.ppermute(share, "tensor", [(i, i ^ 1) for i in range(4)])
    share = share + lax.ppermute(share, "tensor", [(i, i ^ 2) for i in range(4)])
    half = shape(N, 2 * N, dtype=BF16)
    input_grad, gate_grad = call(
        unpack_kernel, (half, half), taken, inputs, gates, out_grad, skip.reshape(1, 2 * N)
    )
    return input_grad, gate_grad, share


def solution(mesh):
    return jax.shard_map(
        local,
        mesh=mesh,
        in_specs=(
            P("context", "tensor"),
            P("context", "tensor"),
            P("context", None),
            P("tensor"),
            P("context", "tensor"),
        ),
        out_specs=(P("context", "tensor"), P("context", "tensor"), P("context", None)),
        check_vma=False,
    )
```

```python
import functools
import math

import jax
import jax.numpy as jnp
import numpy as np
from jax import lax
from jax.experimental import pallas as pl
from jax.experimental.pallas import tpu as pltpu
from jax.sharding import PartitionSpec as P

N = 128
S = 5
F32 = jnp.float32
BF16 = jnp.bfloat16
HBM = pl.BlockSpec(memory_space=pltpu.HBM)


def tables():
    length = N * N
    index = np.arange(N)
    turn = (np.outer(4 * index + 1, index) % (4 * N)) * (2 * math.pi / (4 * N))
    first = [np.cos(turn), -np.sin(turn)]
    scale = 1.0 / (length * math.sqrt(length))
    last = [first[0].T * scale, first[1].T * scale]
    turn = np.outer(4 * index + 1, index) * (2 * math.pi / (4 * length))
    twist = [np.cos(turn), -np.sin(turn)]
    turn = (np.outer(index, index) % N) * (2 * math.pi / N)
    row = [np.cos(turn), -np.sin(turn)]
    return np.stack(first + twist + row + last).astype(np.float32)


def halves(value):
    high = value.astype(BF16)
    return high, (value - high.astype(F32)).astype(BF16)


def dot(a, b):
    return jnp.dot(a, b, preferred_element_type=F32)


def exact_dot(a, b):
    a_high, a_low = halves(a)
    b_high, b_low = halves(b)
    return dot(a_high, b_high) + (dot(a_low, b_high) + dot(a_high, b_low))


def across(*blocks):
    return jnp.concatenate(blocks, axis=1)


def down(*blocks):
    return jnp.concatenate(blocks, axis=0)


def forward(signals, table):
    spec = exact_dot(down(table[0], table[1]), across(*signals))
    tr, ti = table[2], table[3]
    rows = []
    for s in range(len(signals)):
        re, im = spec[:N, s * N : (s + 1) * N], spec[N:, s * N : (s + 1) * N]
        rows.append(across(re * tr - im * ti, re * ti + im * tr))
    rr, ri = table[4], table[5]
    spec = exact_dot(down(*rows), down(across(rr, ri), across(-ri, rr)))
    return [spec[s * N : (s + 1) * N] for s in range(len(signals))]


def inverse(spectra, table):
    rr, ri = table[4], table[5]
    spec = exact_dot(down(*spectra), down(across(rr, -ri), across(ri, rr)))
    tr, ti = table[2], table[3]
    columns = []
    for s in range(len(spectra)):
        re, im = spec[s * N : (s + 1) * N, :N], spec[s * N : (s + 1) * N, N:]
        columns.append(down(re * tr + im * ti, im * tr - re * ti))
    result = exact_dot(across(table[6], table[7]), across(*columns))
    return [result[:, s * N : (s + 1) * N] for s in range(len(spectra))]


def times(a, b):
    ar, ai, br, bi = a[:, :N], a[:, N:], b[:, :N], b[:, N:]
    return across(ar * br - ai * bi, ar * bi + ai * br)


def times_conj(a, b):
    ar, ai, br, bi = a[:, :N], a[:, N:], b[:, :N], b[:, N:]
    return across(ar * br + ai * bi, ai * br - ar * bi)


def core_index():
    return lax.axis_index("tensor") % 2


def signal_rows(ref, s):
    return ref.at[pl.ds(s, N, stride=S), :]


def pack_kernel(
    x_hbm, g_hbm, f_hbm, o_hbm, skip_hbm, out_ref, skip_ref, x_ref, g_ref, f_ref, o_ref, sems
):
    at = pl.multiple_of(core_index() * N, N)
    copies = [
        pltpu.make_async_copy(src, dst, sems.at[i])
        for i, (src, dst) in enumerate(
            [
                (x_hbm, x_ref),
                (f_hbm.at[:, pl.ds(at, N)], f_ref),
                (g_hbm, g_ref),
                (o_hbm, o_ref),
                (skip_hbm, skip_ref),
            ]
        )
    ]
    for copy in copies:
        copy.start()
    copies[0].wait()
    x = x_ref[...].astype(F32)
    for c in range(2):
        signal_rows(out_ref, c)[...] = x[:, c * N : (c + 1) * N].T
    copies[1].wait()
    signal_rows(out_ref, 4)[...] = f_ref[...].T
    copies[2].wait()
    copies[3].wait()
    mixed = o_ref[...].astype(F32) * g_ref[...].astype(F32)
    for c in range(2):
        signal_rows(out_ref, 2 + c)[...] = mixed[:, c * N : (c + 1) * N].T
    copies[4].wait()


def share_kernel(in_ref, table_ref, spec_ref, own_ref, out_ref):
    table = [table_ref[i] for i in range(8)]
    x0, x1, m0, m1 = forward([signal_rows(in_ref, s)[...] for s in range(4)], table)
    for s, spec in enumerate((x0, x1, m0, m1)):
        spec_ref[s] = spec
    share = inverse([times_conj(m0, x0), times_conj(m1, x1)], table)
    first = core_index() == 0
    own_ref[...] = jnp.where(first, share[0], share[1])
    out_ref[:N] = signal_rows(in_ref, 4)[...]
    out_ref[N:] = jnp.where(first, share[1], share[0])


def conv_kernel(spec_ref, own_ref, pair_ref, table_ref, out_ref):
    table = [table_ref[i] for i in range(8)]
    f0, f1 = forward([pair_ref[0, :N], pair_ref[1, :N]], table)
    x0, x1, m0, m1 = (spec_ref[s] for s in range(4))
    results = inverse(
        [times(f0, x0), times(f1, x1), times_conj(m0, f0), times_conj(m1, f1)], table
    )
    for s, result in enumerate(results):
        signal_rows(out_ref, s)[...] = result
    signal_rows(out_ref, 4)[...] = own_ref[...] + pair_ref[1 - core_index(), N:]


def shared_kernel(in_ref, out_ref):
    out_ref[...] = signal_rows(in_ref, 4)[...].T


def unpack_kernel(
    in_ref, all_ref, x_ref, g_ref, o_ref, skip_ref, input_ref, gate_ref, share_ref
):
    for c in range(2):
        at = slice(c * N, (c + 1) * N)
        share_ref[:, at] = all_ref[c] + all_ref[2 + c]
        x = x_ref[:, at].astype(F32)
        upstream = o_ref[:, at].astype(F32)
        mixed = upstream * g_ref[:, at].astype(F32)
        skip = skip_ref[:, at]
        conv = signal_rows(in_ref, c)[...].T
        back = signal_rows(in_ref, 2 + c)[...].T
        input_ref[:, at] = (back + skip * mixed).astype(BF16)
        gate_ref[:, at] = (upstream * (conv + skip * x)).astype(BF16)


def shape(*dims, dtype=F32):
    return jax.ShapeDtypeStruct(dims, dtype)


def call(kernel, out, *operands, **options):
    return pl.pallas_call(
        kernel,
        out_shape=out,
        compiler_params=pltpu.CompilerParams(vmem_limit_bytes=16 << 20),
        **options,
    )(*operands)


def exchange(field):
    field = field.reshape(N, 1, S * N)
    field = lax.all_to_all(field, "context", split_axis=0, concat_axis=0, tiled=True)
    return field.reshape(S * N, N)


def core_groups(size):
    return [[i, i + 1] for i in range(0, size, 2)]


def local(inputs, gates, filters, skip, out_grad):
    tensor = lax.axis_size("tensor")
    table = jnp.asarray(tables())
    sent, skip = call(
        pack_kernel,
        (pltpu.VMEM((S * N, N), F32), pltpu.VMEM((1, 2 * N), F32)),
        *(
            pltpu.with_memory_space_constraint(operand, pltpu.HBM)
            for operand in (inputs, gates, filters, out_grad, skip.reshape(1, 2 * N))
        ),
        in_specs=[HBM] * 5,
        scratch_shapes=[
            pltpu.VMEM((N, 2 * N), BF16),
            pltpu.VMEM((N, 2 * N), BF16),
            pltpu.VMEM((N, N), F32),
            pltpu.VMEM((N, 2 * N), BF16),
            pltpu.SemaphoreType.DMA((5,)),
        ],
    )
    taken = exchange(sent)
    spec, own, pair = call(
        share_kernel, (shape(4, N, 2 * N), shape(N, N), shape(2 * N, N)), taken, table
    )
    pair = lax.all_gather(
        pair, "tensor", axis=0, tiled=False, axis_index_groups=core_groups(tensor)
    )
    sent = call(conv_kernel, shape(S * N, N), spec, own, pair, table)
    taken = exchange(sent)
    share = call(shared_kernel, pltpu.VMEM((N, N), F32), taken)
    share = lax.all_gather(share, "tensor", axis=0, tiled=False)
    half = shape(N, 2 * N, dtype=BF16)
    return call(
        unpack_kernel,
        (half, half, shape(N, 2 * N)),
        taken,
        pltpu.with_memory_space_constraint(share, pltpu.VMEM),
        inputs,
        gates,
        out_grad,
        skip,
    )


def solution(mesh):
    return jax.shard_map(
        local,
        mesh=mesh,
        in_specs=(
            P("context", "tensor"),
            P("context", "tensor"),
            P("context", None),
            P("tensor"),
            P("context", "tensor"),
        ),
        out_specs=(P("context", "tensor"), P("context", "tensor"), P("context", None)),
        check_vma=False,
    )
```

```python
import functools
import math

import jax
import jax.numpy as jnp
import numpy as np
from jax import lax
from jax.experimental import pallas as pl
from jax.experimental.pallas import tpu as pltpu
from jax.sharding import PartitionSpec as P

N = 128
S = 5
F32 = jnp.float32
BF16 = jnp.bfloat16
HBM = pl.BlockSpec(memory_space=pltpu.HBM)


def tables():
    length = N * N
    index = np.arange(N)
    turn = (np.outer(4 * index + 1, index) % (4 * N)) * (2 * math.pi / (4 * N))
    first = [np.cos(turn), -np.sin(turn)]
    scale = 1.0 / (length * math.sqrt(length))
    last = [first[0].T * scale, first[1].T * scale]
    turn = np.outer(4 * index + 1, index) * (2 * math.pi / (4 * length))
    twist = [np.cos(turn), -np.sin(turn)]
    turn = (np.outer(index, index) % N) * (2 * math.pi / N)
    row = [np.cos(turn), -np.sin(turn)]
    return np.stack(first + twist + row + last).astype(np.float32)


def halves(value):
    high = value.astype(BF16)
    return high, (value - high.astype(F32)).astype(BF16)


def dot(a, b):
    return jnp.dot(a, b, preferred_element_type=F32)


def exact_dot(a, b):
    a_high, a_low = halves(a)
    b_high, b_low = halves(b)
    return dot(across(a_high, a_low, a_high), down(b_high, b_high, b_low))


def across(*blocks):
    return jnp.concatenate(blocks, axis=1)


def down(*blocks):
    return jnp.concatenate(blocks, axis=0)


def forward(signals, table):
    spec = exact_dot(down(table[0], table[1]), across(*signals))
    tr, ti = table[2], table[3]
    rows = []
    for s in range(len(signals)):
        re, im = spec[:N, s * N : (s + 1) * N], spec[N:, s * N : (s + 1) * N]
        rows.append(across(re * tr - im * ti, re * ti + im * tr))
    rr, ri = table[4], table[5]
    spec = exact_dot(down(*rows), down(across(rr, ri), across(-ri, rr)))
    return [spec[s * N : (s + 1) * N] for s in range(len(signals))]


def inverse(spectra, table):
    rr, ri = table[4], table[5]
    spec = exact_dot(down(*spectra), down(across(rr, -ri), across(ri, rr)))
    tr, ti = table[2], table[3]
    columns = []
    for s in range(len(spectra)):
        re, im = spec[s * N : (s + 1) * N, :N], spec[s * N : (s + 1) * N, N:]
        columns.append(down(re * tr + im * ti, im * tr - re * ti))
    result = exact_dot(across(table[6], table[7]), across(*columns))
    return [result[:, s * N : (s + 1) * N] for s in range(len(spectra))]


def times(a, b):
    ar, ai, br, bi = a[:, :N], a[:, N:], b[:, :N], b[:, N:]
    return across(ar * br - ai * bi, ar * bi + ai * br)


def times_conj(a, b):
    ar, ai, br, bi = a[:, :N], a[:, N:], b[:, :N], b[:, N:]
    return across(ar * br + ai * bi, ai * br - ar * bi)


def core_index():
    return lax.axis_index("tensor") % 2


def signal_rows(ref, s):
    return ref.at[pl.ds(s, N, stride=S), :]


def pack_kernel(
    x_hbm, g_hbm, f_hbm, o_hbm, skip_hbm, out_ref, skip_ref, x_ref, g_ref, f_ref, o_ref, sems
):
    at = pl.multiple_of(core_index() * N, N)
    copies = [
        pltpu.make_async_copy(src, dst, sems.at[i])
        for i, (src, dst) in enumerate(
            [
                (x_hbm, x_ref),
                (f_hbm.at[:, pl.ds(at, N)], f_ref),
                (g_hbm, g_ref),
                (o_hbm, o_ref),
                (skip_hbm, skip_ref),
            ]
        )
    ]
    for copy in copies:
        copy.start()
    copies[0].wait()
    x = x_ref[...].astype(F32)
    for c in range(2):
        signal_rows(out_ref, c)[...] = x[:, c * N : (c + 1) * N].T
    copies[1].wait()
    signal_rows(out_ref, 4)[...] = f_ref[...].T
    copies[2].wait()
    copies[3].wait()
    mixed = o_ref[...].astype(F32) * g_ref[...].astype(F32)
    for c in range(2):
        signal_rows(out_ref, 2 + c)[...] = mixed[:, c * N : (c + 1) * N].T
    copies[4].wait()


def share_kernel(in_ref, table_ref, spec_ref, own_ref, out_ref):
    table = [table_ref[i] for i in range(8)]
    x0, x1, m0, m1, f = forward([signal_rows(in_ref, s)[...] for s in range(S)], table)
    for s, spec in enumerate((x0, x1, m0, m1)):
        spec_ref[s] = spec
    share = inverse([times_conj(m0, x0), times_conj(m1, x1)], table)
    first = core_index() == 0
    own_ref[...] = jnp.where(first, share[0], share[1])
    out_ref[0] = f[:, :N]
    out_ref[1] = f[:, N:]
    out_ref[2] = jnp.where(first, share[1], share[0])


def conv_kernel(spec_ref, own_ref, pair_ref, table_ref, out_ref):
    table = [table_ref[i] for i in range(8)]
    f0, f1 = (across(pair_ref[c, 0], pair_ref[c, 1]) for c in range(2))
    x0, x1, m0, m1 = (spec_ref[s] for s in range(4))
    results = inverse(
        [times(f0, x0), times(f1, x1), times_conj(m0, f0), times_conj(m1, f1)], table
    )
    for s, result in enumerate(results):
        signal_rows(out_ref, s)[...] = result
    signal_rows(out_ref, 4)[...] = own_ref[...] + pair_ref[1 - core_index(), 2]


def shared_kernel(in_ref, out_ref):
    out_ref[...] = signal_rows(in_ref, 4)[...].T


def unpack_kernel(
    in_ref, all_ref, x_ref, g_ref, o_ref, skip_ref, input_ref, gate_ref, share_ref
):
    for c in range(2):
        at = slice(c * N, (c + 1) * N)
        share_ref[:, at] = all_ref[c] + all_ref[2 + c]
        x = x_ref[:, at].astype(F32)
        upstream = o_ref[:, at].astype(F32)
        mixed = upstream * g_ref[:, at].astype(F32)
        skip = skip_ref[:, at]
        conv = signal_rows(in_ref, c)[...].T
        back = signal_rows(in_ref, 2 + c)[...].T
        input_ref[:, at] = (back + skip * mixed).astype(BF16)
        gate_ref[:, at] = (upstream * (conv + skip * x)).astype(BF16)


def shape(*dims, dtype=F32):
    return jax.ShapeDtypeStruct(dims, dtype)


def call(kernel, out, *operands, **options):
    return pl.pallas_call(
        kernel,
        out_shape=out,
        compiler_params=pltpu.CompilerParams(vmem_limit_bytes=16 << 20),
        **options,
    )(*operands)


def exchange(field):
    field = field.reshape(N, 1, S * N)
    field = lax.all_to_all(field, "context", split_axis=0, concat_axis=0, tiled=True)
    return field.reshape(S * N, N)


def core_groups(size):
    return [[i, i + 1] for i in range(0, size, 2)]


def local(inputs, gates, filters, skip, out_grad):
    tensor = lax.axis_size("tensor")
    table = jnp.asarray(tables())
    sent, skip = call(
        pack_kernel,
        (pltpu.VMEM((S * N, N), F32), pltpu.VMEM((1, 2 * N), F32)),
        *(
            pltpu.with_memory_space_constraint(operand, pltpu.HBM)
            for operand in (inputs, gates, filters, out_grad, skip.reshape(1, 2 * N))
        ),
        in_specs=[HBM] * 5,
        scratch_shapes=[
            pltpu.VMEM((N, 2 * N), BF16),
            pltpu.VMEM((N, 2 * N), BF16),
            pltpu.VMEM((N, N), F32),
            pltpu.VMEM((N, 2 * N), BF16),
            pltpu.SemaphoreType.DMA((5,)),
        ],
    )
    taken = exchange(sent)
    spec, own, pair = call(
        share_kernel, (shape(4, N, 2 * N), shape(N, N), shape(3, N, N)), taken, table
    )
    pair = lax.all_gather(
        pair, "tensor", axis=0, tiled=False, axis_index_groups=core_groups(tensor)
    )
    sent = call(conv_kernel, shape(S * N, N), spec, own, pair, table)
    taken = exchange(sent)
    share = call(shared_kernel, pltpu.VMEM((N, N), F32), taken)
    share = lax.all_gather(share, "tensor", axis=0, tiled=False)
    half = shape(N, 2 * N, dtype=BF16)
    return call(
        unpack_kernel,
        (half, half, shape(N, 2 * N)),
        taken,
        pltpu.with_memory_space_constraint(share, pltpu.VMEM),
        inputs,
        gates,
        out_grad,
        skip,
    )


def solution(mesh):
    return jax.shard_map(
        local,
        mesh=mesh,
        in_specs=(
            P("context", "tensor"),
            P("context", "tensor"),
            P("context", None),
            P("tensor"),
            P("context", "tensor"),
        ),
        out_specs=(P("context", "tensor"), P("context", "tensor"), P("context", None)),
        check_vma=False,
    )
```

```python
import functools
import math

import jax
import jax.numpy as jnp
import numpy as np
from jax import lax
from jax.experimental import pallas as pl
from jax.experimental.pallas import tpu as pltpu
from jax.sharding import PartitionSpec as P

N = 128
S = 5
F32 = jnp.float32
BF16 = jnp.bfloat16
HBM = pl.BlockSpec(memory_space=pltpu.HBM)


def partners():
    return np.random.default_rng(16).permutation(N)


def tables():
    length = N * N
    index = np.arange(N)
    turn = (np.outer(4 * index + 1, partners()) % (4 * N)) * (2 * math.pi / (4 * N))
    first = [np.cos(turn), -np.sin(turn)]
    scale = 1.0 / (length * math.sqrt(length))
    last = [first[0].T * scale, first[1].T * scale]
    turn = np.outer(4 * index + 1, index) * (2 * math.pi / (4 * length))
    twist = [np.cos(turn), -np.sin(turn)]
    turn = (np.outer(index, index) % N) * (2 * math.pi / N)
    row = [np.cos(turn), -np.sin(turn)]
    return np.stack(first + twist + row + last).astype(np.float32)


def halves(value):
    high = value.astype(BF16)
    return high, (value - high.astype(F32)).astype(BF16)


def dot(a, b):
    return jnp.dot(a, b, preferred_element_type=F32)


def exact_dot(a, b):
    a_high, a_low = halves(a)
    b_high, b_low = halves(b)
    return dot(across(a_high, a_low, a_high), down(b_high, b_high, b_low))


def across(*blocks):
    return jnp.concatenate(blocks, axis=1)


def down(*blocks):
    return jnp.concatenate(blocks, axis=0)


def forward(signals, table):
    spec = exact_dot(down(table[0], table[1]), across(*signals))
    tr, ti = table[2], table[3]
    rows = []
    for s in range(len(signals)):
        re, im = spec[:N, s * N : (s + 1) * N], spec[N:, s * N : (s + 1) * N]
        rows.append(across(re * tr - im * ti, re * ti + im * tr))
    rr, ri = table[4], table[5]
    spec = exact_dot(down(*rows), down(across(rr, ri), across(-ri, rr)))
    return [spec[s * N : (s + 1) * N] for s in range(len(signals))]


def inverse(spectra, table):
    rr, ri = table[4], table[5]
    spec = exact_dot(down(*spectra), down(across(rr, -ri), across(ri, rr)))
    tr, ti = table[2], table[3]
    columns = []
    for s in range(len(spectra)):
        re, im = spec[s * N : (s + 1) * N, :N], spec[s * N : (s + 1) * N, N:]
        columns.append(down(re * tr + im * ti, im * tr - re * ti))
    result = exact_dot(across(table[6], table[7]), across(*columns))
    return [result[:, s * N : (s + 1) * N] for s in range(len(spectra))]


def times(a, b):
    ar, ai, br, bi = a[:, :N], a[:, N:], b[:, :N], b[:, N:]
    return across(ar * br - ai * bi, ar * bi + ai * br)


def times_conj(a, b):
    ar, ai, br, bi = a[:, :N], a[:, N:], b[:, :N], b[:, N:]
    return across(ar * br + ai * bi, ai * br - ar * bi)


def core_index():
    return lax.axis_index("tensor") % 2


def signal_rows(ref, s):
    return ref.at[pl.ds(s, N, stride=S), :]


def pack_kernel(
    x_hbm, g_hbm, f_hbm, o_hbm, skip_hbm, out_ref, skip_ref, x_ref, g_ref, f_ref, o_ref, sems
):
    at = pl.multiple_of(core_index() * N, N)
    copies = [
        pltpu.make_async_copy(src, dst, sems.at[i])
        for i, (src, dst) in enumerate(
            [
                (g_hbm, g_ref),
                (o_hbm, o_ref),
                (x_hbm, x_ref),
                (f_hbm.at[:, pl.ds(at, N)], f_ref),
                (skip_hbm, skip_ref),
            ]
        )
    ]
    for copy in copies:
        copy.start()
    copies[0].wait()
    copies[1].wait()
    mixed = o_ref[...].astype(F32) * g_ref[...].astype(F32)
    for c in range(2):
        signal_rows(out_ref, 2 + c)[...] = mixed[:, c * N : (c + 1) * N].T
    copies[2].wait()
    x = x_ref[...].astype(F32)
    for c in range(2):
        signal_rows(out_ref, c)[...] = x[:, c * N : (c + 1) * N].T
    copies[3].wait()
    signal_rows(out_ref, 4)[...] = f_ref[...].T
    copies[4].wait()


def spectra_kernel(in_ref, table_ref, spec_ref, own_ref, out_ref):
    table = [table_ref[i] for i in range(8)]
    x0, x1, m0, m1, f = forward([signal_rows(in_ref, s)[...] for s in range(S)], table)
    for s, spec in enumerate((x0, x1, m0, m1)):
        spec_ref[s] = spec
    share = times_conj(m0, x0), times_conj(m1, x1)
    first = core_index() == 0
    own_ref[...] = jnp.where(first, share[0], share[1])
    out_ref[0] = f
    out_ref[1] = jnp.where(first, share[1], share[0])


def inverse_kernel(spec_ref, own_ref, pair_ref, table_ref, out_ref):
    table = [table_ref[i] for i in range(8)]
    f0, f1 = pair_ref[0, 0], pair_ref[1, 0]
    x0, x1, m0, m1 = (spec_ref[s] for s in range(4))
    share = own_ref[...] + pair_ref[1 - core_index(), 1]
    results = inverse(
        [times(f0, x0), times(f1, x1), times_conj(m0, f0), times_conj(m1, f1), share], table
    )
    for s, result in enumerate(results):
        signal_rows(out_ref, s)[...] = result


def shared_kernel(in_ref, out_ref):
    out_ref[...] = signal_rows(in_ref, 4)[...].T


def unpack_kernel(
    in_ref,
    all_ref,
    x_ref,
    g_ref,
    o_ref,
    skip_ref,
    input_hbm,
    gate_hbm,
    share_hbm,
    input_ref,
    gate_ref,
    share_ref,
    sems,
):
    copies = [
        pltpu.make_async_copy(src, dst, sems.at[i])
        for i, (src, dst) in enumerate(
            [(share_ref, share_hbm), (input_ref, input_hbm), (gate_ref, gate_hbm)]
        )
    ]
    halves_of = [slice(c * N, (c + 1) * N) for c in range(2)]
    for c, at in enumerate(halves_of):
        share_ref[:, at] = all_ref[c] + all_ref[2 + c]
    copies[0].start()
    for c, at in enumerate(halves_of):
        back = signal_rows(in_ref, 2 + c)[...].T
        mixed = o_ref[:, at].astype(F32) * g_ref[:, at].astype(F32)
        input_ref[:, at] = (back + skip_ref[:, at] * mixed).astype(BF16)
    copies[1].start()
    for c, at in enumerate(halves_of):
        conv = signal_rows(in_ref, c)[...].T
        x = x_ref[:, at].astype(F32)
        gate_ref[:, at] = (o_ref[:, at].astype(F32) * (conv + skip_ref[:, at] * x)).astype(BF16)
    copies[2].start()
    for copy in copies:
        copy.wait()


def shape(*dims, dtype=F32):
    return jax.ShapeDtypeStruct(dims, dtype)


def call(kernel, out, *operands, **options):
    return pl.pallas_call(
        kernel,
        out_shape=out,
        compiler_params=pltpu.CompilerParams(vmem_limit_bytes=16 << 20),
        **options,
    )(*operands)


def exchange(field):
    field = field.reshape(N, 1, S * N)
    field = lax.all_to_all(
        field,
        "context",
        split_axis=0,
        concat_axis=0,
        tiled=True,
        axis_index_groups=[partners().tolist()],
    )
    return field.reshape(S * N, N)


def core_groups(size):
    return [[i, i + 1] for i in range(0, size, 2)]


def local(inputs, gates, filters, skip, out_grad):
    tensor = lax.axis_size("tensor")
    table = jnp.asarray(tables())
    sent, skip = call(
        pack_kernel,
        (pltpu.VMEM((S * N, N), F32), pltpu.VMEM((1, 2 * N), F32)),
        *(
            pltpu.with_memory_space_constraint(operand, pltpu.HBM)
            for operand in (inputs, gates, filters, out_grad, skip.reshape(1, 2 * N))
        ),
        in_specs=[HBM] * 5,
        scratch_shapes=[
            pltpu.VMEM((N, 2 * N), BF16),
            pltpu.VMEM((N, 2 * N), BF16),
            pltpu.VMEM((N, N), F32),
            pltpu.VMEM((N, 2 * N), BF16),
            pltpu.SemaphoreType.DMA((5,)),
        ],
    )
    taken = exchange(sent)
    spec, own, pair = call(
        spectra_kernel,
        (shape(4, N, 2 * N), shape(N, 2 * N), shape(2, N, 2 * N)),
        taken,
        table,
    )
    pair = lax.all_gather(
        pair, "tensor", axis=0, tiled=False, axis_index_groups=core_groups(tensor)
    )
    sent = call(inverse_kernel, shape(S * N, N), spec, own, pair, table)
    taken = exchange(sent)
    share = call(shared_kernel, pltpu.VMEM((N, N), F32), taken)
    share = lax.all_gather(share, "tensor", axis=0, tiled=False)
    half = shape(N, 2 * N, dtype=BF16)
    return call(
        unpack_kernel,
        (half, half, shape(N, 2 * N)),
        taken,
        pltpu.with_memory_space_constraint(share, pltpu.VMEM),
        inputs,
        gates,
        out_grad,
        skip,
        out_specs=(HBM,) * 3,
        scratch_shapes=[
            pltpu.VMEM((N, 2 * N), BF16),
            pltpu.VMEM((N, 2 * N), BF16),
            pltpu.VMEM((N, 2 * N), F32),
            pltpu.SemaphoreType.DMA((3,)),
        ],
    )


def solution(mesh):
    return jax.shard_map(
        local,
        mesh=mesh,
        in_specs=(
            P("context", "tensor"),
            P("context", "tensor"),
            P("context", None),
            P("tensor"),
            P("context", "tensor"),
        ),
        out_specs=(P("context", "tensor"), P("context", "tensor"), P("context", None)),
        check_vma=False,
    )
```

```python
import functools
import math

import jax
import jax.numpy as jnp
import numpy as np
from jax import lax
from jax.experimental import pallas as pl
from jax.experimental.pallas import tpu as pltpu
from jax.sharding import PartitionSpec as P

N = 128
S = 5
F32 = jnp.float32
BF16 = jnp.bfloat16
HBM = pl.BlockSpec(memory_space=pltpu.HBM)


def partners():
    return np.random.default_rng(52).permutation(N)


def tables():
    length = N * N
    index = np.arange(N)
    turn = (np.outer(4 * index + 1, partners()) % (4 * N)) * (2 * math.pi / (4 * N))
    first = [np.cos(turn), -np.sin(turn)]
    scale = 1.0 / (length * math.sqrt(length))
    last = [first[0].T * scale, first[1].T * scale]
    turn = np.outer(4 * index + 1, index) * (2 * math.pi / (4 * length))
    twist = [np.cos(turn), -np.sin(turn)]
    turn = (np.outer(index, index) % N) * (2 * math.pi / N)
    row = [np.cos(turn), -np.sin(turn)]
    return np.stack(first + twist + row + last).astype(np.float32)


def halves(value):
    high = value.astype(BF16)
    return high, (value - high.astype(F32)).astype(BF16)


def dot(a, b):
    return jnp.dot(a, b, preferred_element_type=F32)


def exact_dot(a, b):
    a_high, a_low = halves(a)
    b_high, b_low = halves(b)
    return dot(across(a_high, a_low, a_high), down(b_high, b_high, b_low))


def across(*blocks):
    return jnp.concatenate(blocks, axis=1)


def down(*blocks):
    return jnp.concatenate(blocks, axis=0)


def forward(signals, table):
    spec = exact_dot(down(table[0], table[1]), across(*signals))
    tr, ti = table[2], table[3]
    rows = []
    for s in range(len(signals)):
        re, im = spec[:N, s * N : (s + 1) * N], spec[N:, s * N : (s + 1) * N]
        rows.append(across(re * tr - im * ti, re * ti + im * tr))
    rr, ri = table[4], table[5]
    spec = exact_dot(down(*rows), down(across(rr, ri), across(-ri, rr)))
    return [spec[s * N : (s + 1) * N] for s in range(len(signals))]


def inverse(spectra, table):
    rr, ri = table[4], table[5]
    spec = exact_dot(down(*spectra), down(across(rr, -ri), across(ri, rr)))
    tr, ti = table[2], table[3]
    columns = []
    for s in range(len(spectra)):
        re, im = spec[s * N : (s + 1) * N, :N], spec[s * N : (s + 1) * N, N:]
        columns.append(down(re * tr + im * ti, im * tr - re * ti))
    result = exact_dot(across(table[6], table[7]), across(*columns))
    return [result[:, s * N : (s + 1) * N] for s in range(len(spectra))]


def times(a, b):
    ar, ai, br, bi = a[:, :N], a[:, N:], b[:, :N], b[:, N:]
    return across(ar * br - ai * bi, ar * bi + ai * br)


def times_conj(a, b):
    ar, ai, br, bi = a[:, :N], a[:, N:], b[:, :N], b[:, N:]
    return across(ar * br + ai * bi, ai * br - ar * bi)


def core_index():
    return lax.axis_index("tensor") % 2


def signal_rows(ref, s):
    return ref.at[pl.ds(s, N, stride=S), :]


def pack_kernel(
    x_hbm, g_hbm, f_hbm, o_hbm, skip_hbm, out_ref, skip_ref, x_ref, g_ref, f_ref, o_ref, sems
):
    at = pl.multiple_of(core_index() * N, N)
    copies = [
        pltpu.make_async_copy(src, dst, sems.at[i])
        for i, (src, dst) in enumerate(
            [
                (g_hbm, g_ref),
                (o_hbm, o_ref),
                (x_hbm, x_ref),
                (f_hbm.at[:, pl.ds(at, N)], f_ref),
                (skip_hbm, skip_ref),
            ]
        )
    ]
    for copy in copies:
        copy.start()
    copies[0].wait()
    copies[1].wait()
    mixed = o_ref[...].astype(F32) * g_ref[...].astype(F32)
    for c in range(2):
        signal_rows(out_ref, 2 + c)[...] = mixed[:, c * N : (c + 1) * N].T
    copies[2].wait()
    x = x_ref[...].astype(F32)
    for c in range(2):
        signal_rows(out_ref, c)[...] = x[:, c * N : (c + 1) * N].T
    copies[3].wait()
    signal_rows(out_ref, 4)[...] = f_ref[...].T
    copies[4].wait()


def spectra_kernel(in_ref, table_ref, spec_ref, own_ref, out_ref):
    table = [table_ref[i] for i in range(8)]
    x0, x1, m0, m1, f = forward([signal_rows(in_ref, s)[...] for s in range(S)], table)
    for s, spec in enumerate((x0, x1, m0, m1)):
        spec_ref[s] = spec
    share = times_conj(m0, x0), times_conj(m1, x1)
    first = core_index() == 0
    own_ref[...] = jnp.where(first, share[0], share[1])
    out_ref[0] = f
    out_ref[1] = jnp.where(first, share[1], share[0])


def inverse_kernel(spec_ref, own_ref, pair_ref, table_ref, out_ref):
    table = [table_ref[i] for i in range(8)]
    f0, f1 = pair_ref[0, 0], pair_ref[1, 0]
    x0, x1, m0, m1 = (spec_ref[s] for s in range(4))
    share = own_ref[...] + pair_ref[1 - core_index(), 1]
    results = inverse(
        [times(f0, x0), times(f1, x1), times_conj(m0, f0), times_conj(m1, f1), share], table
    )
    for s, result in enumerate(results):
        signal_rows(out_ref, s)[...] = result


def shared_kernel(in_ref, out_ref):
    out_ref[...] = signal_rows(in_ref, 4)[...].T


def unpack_kernel(
    in_ref,
    all_ref,
    x_ref,
    g_ref,
    o_ref,
    skip_ref,
    input_hbm,
    gate_hbm,
    share_hbm,
    input_ref,
    gate_ref,
    share_ref,
    sems,
):
    copies = [
        pltpu.make_async_copy(src, dst, sems.at[i])
        for i, (src, dst) in enumerate(
            [(share_ref, share_hbm), (input_ref, input_hbm), (gate_ref, gate_hbm)]
        )
    ]
    halves_of = [slice(c * N, (c + 1) * N) for c in range(2)]
    for c, at in enumerate(halves_of):
        share_ref[:, at] = all_ref[c] + all_ref[2 + c]
    copies[0].start()
    for c, at in enumerate(halves_of):
        back = signal_rows(in_ref, 2 + c)[...].T
        mixed = o_ref[:, at].astype(F32) * g_ref[:, at].astype(F32)
        input_ref[:, at] = (back + skip_ref[:, at] * mixed).astype(BF16)
    copies[1].start()
    for c, at in enumerate(halves_of):
        conv = signal_rows(in_ref, c)[...].T
        x = x_ref[:, at].astype(F32)
        gate_ref[:, at] = (o_ref[:, at].astype(F32) * (conv + skip_ref[:, at] * x)).astype(BF16)
    copies[2].start()
    for copy in copies:
        copy.wait()


def shape(*dims, dtype=F32):
    return jax.ShapeDtypeStruct(dims, dtype)


def call(kernel, out, *operands, **options):
    return pl.pallas_call(
        kernel,
        out_shape=out,
        compiler_params=pltpu.CompilerParams(vmem_limit_bytes=16 << 20),
        **options,
    )(*operands)


def exchange(field):
    field = field.reshape(N, 1, S * N)
    field = lax.all_to_all(
        field,
        "context",
        split_axis=0,
        concat_axis=0,
        tiled=True,
        axis_index_groups=[partners().tolist()],
    )
    return field.reshape(S * N, N)


def core_groups(size):
    return [[i, i + 1] for i in range(0, size, 2)]


def local(inputs, gates, filters, skip, out_grad):
    tensor = lax.axis_size("tensor")
    table = jnp.asarray(tables())
    sent, skip = call(
        pack_kernel,
        (pltpu.VMEM((S * N, N), F32), pltpu.VMEM((1, 2 * N), F32)),
        *(
            pltpu.with_memory_space_constraint(operand, pltpu.HBM)
            for operand in (inputs, gates, filters, out_grad, skip.reshape(1, 2 * N))
        ),
        in_specs=[HBM] * 5,
        scratch_shapes=[
            pltpu.VMEM((N, 2 * N), BF16),
            pltpu.VMEM((N, 2 * N), BF16),
            pltpu.VMEM((N, N), F32),
            pltpu.VMEM((N, 2 * N), BF16),
            pltpu.SemaphoreType.DMA((5,)),
        ],
    )
    taken = exchange(sent)
    spec, own, pair = call(
        spectra_kernel,
        (shape(4, N, 2 * N), shape(N, 2 * N), shape(2, N, 2 * N)),
        taken,
        table,
    )
    pair = lax.all_gather(
        pair, "tensor", axis=0, tiled=False, axis_index_groups=core_groups(tensor)
    )
    sent = call(inverse_kernel, shape(S * N, N), spec, own, pair, table)
    taken = exchange(sent)
    share = call(shared_kernel, pltpu.VMEM((N, N), F32), taken)
    share = lax.all_gather(share, "tensor", axis=0, tiled=False)
    half = shape(N, 2 * N, dtype=BF16)
    return call(
        unpack_kernel,
        (half, half, shape(N, 2 * N)),
        taken,
        pltpu.with_memory_space_constraint(share, pltpu.VMEM),
        inputs,
        gates,
        out_grad,
        skip,
        out_specs=(HBM,) * 3,
        scratch_shapes=[
            pltpu.VMEM((N, 2 * N), BF16),
            pltpu.VMEM((N, 2 * N), BF16),
            pltpu.VMEM((N, 2 * N), F32),
            pltpu.SemaphoreType.DMA((3,)),
        ],
    )


def solution(mesh):
    return jax.shard_map(
        local,
        mesh=mesh,
        in_specs=(
            P("context", "tensor"),
            P("context", "tensor"),
            P("context", None),
            P("tensor"),
            P("context", "tensor"),
        ),
        out_specs=(P("context", "tensor"), P("context", "tensor"), P("context", None)),
        check_vma=False,
    )
```

```python
import functools
import math

import jax
import jax.numpy as jnp
import numpy as np
from jax import lax
from jax.experimental import pallas as pl
from jax.experimental.pallas import tpu as pltpu
from jax.sharding import PartitionSpec as P

N = 128
S = 5
F32 = jnp.float32
BF16 = jnp.bfloat16
HBM = pl.BlockSpec(memory_space=pltpu.HBM)


def partners(side):
    return np.random.default_rng((52, 59)[side]).permutation(N)


def tables(side):
    length = N * N
    index = np.arange(N)
    turn = (np.outer(4 * index + 1, partners(side)) % (4 * N)) * (2 * math.pi / (4 * N))
    first = [np.cos(turn), -np.sin(turn)]
    scale = 1.0 / (length * math.sqrt(length))
    last = [first[0].T * scale, first[1].T * scale]
    turn = np.outer(4 * index + 1, index) * (2 * math.pi / (4 * length))
    twist = [np.cos(turn), -np.sin(turn)]
    turn = (np.outer(index, index) % N) * (2 * math.pi / N)
    row = [np.cos(turn), -np.sin(turn)]
    return np.stack(first + twist + row + last).astype(np.float32)


def halves(value):
    high = value.astype(BF16)
    return high, (value - high.astype(F32)).astype(BF16)


def dot(a, b):
    return jnp.dot(a, b, preferred_element_type=F32)


def exact_dot(a, b):
    a_high, a_low = halves(a)
    b_high, b_low = halves(b)
    return dot(across(a_high, a_low, a_high), down(b_high, b_high, b_low))


def across(*blocks):
    return jnp.concatenate(blocks, axis=1)


def down(*blocks):
    return jnp.concatenate(blocks, axis=0)


def forward(signals, table):
    spec = exact_dot(down(table[0], table[1]), across(*signals))
    tr, ti = table[2], table[3]
    rows = []
    for s in range(len(signals)):
        re, im = spec[:N, s * N : (s + 1) * N], spec[N:, s * N : (s + 1) * N]
        rows.append(across(re * tr - im * ti, re * ti + im * tr))
    rr, ri = table[4], table[5]
    spec = exact_dot(down(*rows), down(across(rr, ri), across(-ri, rr)))
    return [spec[s * N : (s + 1) * N] for s in range(len(signals))]


def inverse(spectra, table):
    rr, ri = table[4], table[5]
    spec = exact_dot(down(*spectra), down(across(rr, -ri), across(ri, rr)))
    tr, ti = table[2], table[3]
    columns = []
    for s in range(len(spectra)):
        re, im = spec[s * N : (s + 1) * N, :N], spec[s * N : (s + 1) * N, N:]
        columns.append(down(re * tr + im * ti, im * tr - re * ti))
    result = exact_dot(across(table[6], table[7]), across(*columns))
    return [result[:, s * N : (s + 1) * N] for s in range(len(spectra))]


def times(a, b):
    ar, ai, br, bi = a[:, :N], a[:, N:], b[:, :N], b[:, N:]
    return across(ar * br - ai * bi, ar * bi + ai * br)


def times_conj(a, b):
    ar, ai, br, bi = a[:, :N], a[:, N:], b[:, :N], b[:, N:]
    return across(ar * br + ai * bi, ai * br - ar * bi)


def core_index():
    return lax.axis_index("tensor") % 2


def signal_rows(ref, s):
    return ref.at[pl.ds(s, N, stride=S), :]


def pack_kernel(
    x_hbm, g_hbm, f_hbm, o_hbm, skip_hbm, out_ref, skip_ref, x_ref, g_ref, f_ref, o_ref, sems
):
    at = pl.multiple_of(core_index() * N, N)
    copies = [
        pltpu.make_async_copy(src, dst, sems.at[i])
        for i, (src, dst) in enumerate(
            [
                (g_hbm, g_ref),
                (o_hbm, o_ref),
                (x_hbm, x_ref),
                (f_hbm.at[:, pl.ds(at, N)], f_ref),
                (skip_hbm, skip_ref),
            ]
        )
    ]
    for copy in copies:
        copy.start()
    copies[0].wait()
    copies[1].wait()
    mixed = o_ref[...].astype(F32) * g_ref[...].astype(F32)
    for c in range(2):
        signal_rows(out_ref, 2 + c)[...] = mixed[:, c * N : (c + 1) * N].T
    copies[2].wait()
    x = x_ref[...].astype(F32)
    for c in range(2):
        signal_rows(out_ref, c)[...] = x[:, c * N : (c + 1) * N].T
    copies[3].wait()
    signal_rows(out_ref, 4)[...] = f_ref[...].T
    copies[4].wait()


def spectra_kernel(in_ref, table_ref, spec_ref, own_ref, out_ref):
    side = lax.axis_index("tensor") // 2
    table = [table_ref[side, i] for i in range(8)]
    x0, x1, m0, m1, f = forward([signal_rows(in_ref, s)[...] for s in range(S)], table)
    for s, spec in enumerate((x0, x1, m0, m1)):
        spec_ref[s] = spec
    share = times_conj(m0, x0), times_conj(m1, x1)
    first = core_index() == 0
    own_ref[...] = jnp.where(first, share[0], share[1])
    out_ref[0] = f
    out_ref[1] = jnp.where(first, share[1], share[0])


def inverse_kernel(spec_ref, own_ref, pair_ref, table_ref, out_ref):
    side = lax.axis_index("tensor") // 2
    table = [table_ref[side, i] for i in range(8)]
    f0, f1 = pair_ref[0, 0], pair_ref[1, 0]
    x0, x1, m0, m1 = (spec_ref[s] for s in range(4))
    share = own_ref[...] + pair_ref[1 - core_index(), 1]
    results = inverse(
        [times(f0, x0), times(f1, x1), times_conj(m0, f0), times_conj(m1, f1), share], table
    )
    for s, result in enumerate(results):
        signal_rows(out_ref, s)[...] = result


def shared_kernel(in_ref, out_ref):
    out_ref[...] = signal_rows(in_ref, 4)[...].T


def unpack_kernel(
    in_ref,
    all_ref,
    x_ref,
    g_ref,
    o_ref,
    skip_ref,
    input_hbm,
    gate_hbm,
    share_hbm,
    input_ref,
    gate_ref,
    share_ref,
    sems,
):
    copies = [
        pltpu.make_async_copy(src, dst, sems.at[i])
        for i, (src, dst) in enumerate(
            [(share_ref, share_hbm), (input_ref, input_hbm), (gate_ref, gate_hbm)]
        )
    ]
    halves_of = [slice(c * N, (c + 1) * N) for c in range(2)]
    for c, at in enumerate(halves_of):
        share_ref[:, at] = all_ref[c] + all_ref[2 + c]
    copies[0].start()
    for c, at in enumerate(halves_of):
        back = signal_rows(in_ref, 2 + c)[...].T
        mixed = o_ref[:, at].astype(F32) * g_ref[:, at].astype(F32)
        input_ref[:, at] = (back + skip_ref[:, at] * mixed).astype(BF16)
    copies[1].start()
    for c, at in enumerate(halves_of):
        conv = signal_rows(in_ref, c)[...].T
        x = x_ref[:, at].astype(F32)
        gate_ref[:, at] = (o_ref[:, at].astype(F32) * (conv + skip_ref[:, at] * x)).astype(BF16)
    copies[2].start()
    for copy in copies:
        copy.wait()


def shape(*dims, dtype=F32):
    return jax.ShapeDtypeStruct(dims, dtype)


def call(kernel, out, *operands, **options):
    return pl.pallas_call(
        kernel,
        out_shape=out,
        compiler_params=pltpu.CompilerParams(vmem_limit_bytes=16 << 20),
        **options,
    )(*operands)


def exchange(field):
    field = field.reshape(N, 1, S * N)
    field = lax.all_to_all(
        field,
        ("tensor", "context"),
        split_axis=0,
        concat_axis=0,
        tiled=True,
        axis_index_groups=[(t * N + partners(t // 2)).tolist() for t in range(4)],
    )
    return field.reshape(S * N, N)


def core_groups(size):
    return [[i, i + 1] for i in range(0, size, 2)]


def local(inputs, gates, filters, skip, out_grad):
    tensor = lax.axis_size("tensor")
    table = jnp.asarray(np.stack([tables(0), tables(1)]))
    sent, skip = call(
        pack_kernel,
        (pltpu.VMEM((S * N, N), F32), pltpu.VMEM((1, 2 * N), F32)),
        *(
            pltpu.with_memory_space_constraint(operand, pltpu.HBM)
            for operand in (inputs, gates, filters, out_grad, skip.reshape(1, 2 * N))
        ),
        in_specs=[HBM] * 5,
        scratch_shapes=[
            pltpu.VMEM((N, 2 * N), BF16),
            pltpu.VMEM((N, 2 * N), BF16),
            pltpu.VMEM((N, N), F32),
            pltpu.VMEM((N, 2 * N), BF16),
            pltpu.SemaphoreType.DMA((5,)),
        ],
    )
    taken = exchange(sent)
    spec, own, pair = call(
        spectra_kernel,
        (shape(4, N, 2 * N), shape(N, 2 * N), shape(2, N, 2 * N)),
        taken,
        table,
    )
    pair = lax.all_gather(
        pair, "tensor", axis=0, tiled=False, axis_index_groups=core_groups(tensor)
    )
    sent = call(inverse_kernel, shape(S * N, N), spec, own, pair, table)
    taken = exchange(sent)
    share = call(shared_kernel, pltpu.VMEM((N, N), F32), taken)
    share = lax.all_gather(share, "tensor", axis=0, tiled=False)
    half = shape(N, 2 * N, dtype=BF16)
    return call(
        unpack_kernel,
        (half, half, shape(N, 2 * N)),
        taken,
        pltpu.with_memory_space_constraint(share, pltpu.VMEM),
        inputs,
        gates,
        out_grad,
        skip,
        out_specs=(HBM,) * 3,
        scratch_shapes=[
            pltpu.VMEM((N, 2 * N), BF16),
            pltpu.VMEM((N, 2 * N), BF16),
            pltpu.VMEM((N, 2 * N), F32),
            pltpu.SemaphoreType.DMA((3,)),
        ],
    )


def solution(mesh):
    return jax.shard_map(
        local,
        mesh=mesh,
        in_specs=(
            P("context", "tensor"),
            P("context", "tensor"),
            P("context", None),
            P("tensor"),
            P("context", "tensor"),
        ),
        out_specs=(P("context", "tensor"), P("context", "tensor"), P("context", None)),
        check_vma=False,
    )
```
